32 devices in a mesh: req: 8 (over z, x), head: 4 (over y, core).
Axes of the slice: x: 2, y: 2, z: 4, core: 2. Of those that a mesh axis runs over, the one named last changes fastest.
Arguments:
- tokens: bfloat16 [8192, 1536], P(('req', 'head')), may hold values from -6 to 6
- norm1_gain: float32 [1536], replicated, may hold values from 0.1 to 1.9
- query_key_value_weight: bfloat16 [1536, 2048], replicated, may hold values from -0.15625 to 0.15625
- w_out: bfloat16 [1536, 1536], replicated, may hold values from -0.15625 to 0.15625
- norm2_gain: float32 [1536], replicated, may hold values from 0.1 to 1.9
- router_weight: float32 [1536, 8], replicated, may hold values from -0.078125 to 0.078125
- w_gate_up: bfloat16 [8, 1536, 1536], P('req'), may hold values from -0.15625 to 0.15625
- w_down: bfloat16 [8, 768, 1536], P('req'), may hold values from -0.21875 to 0.21875
- routes: int32 [8192, 4], P(('req', 'head')), may hold values from 0 to 7, all different within a row; in each aligned block of 256 rows (0 to 255, 256 to 511, ...) at most 192 rows name the same one
- key_page_store: bfloat16 [256, 128, 256], P('req'), may hold values from -100 to 100
- value_page_store: bfloat16 [256, 128, 256], P('req'), may hold values from -6 to 6
- page_table: int32 [16, 16], P('req'), may hold values from 0 to 31, as said below
- cached_pages: int32 [16], replicated, may hold values from 0 to 16
- anchor: int32 [16], replicated, may hold values from 0 to 15, as said below
Outputs:
- mixed: bfloat16 [8192, 1536], P(('req', 'head'))
- appended: bfloat16 [8192, 512], P(('req', 'head'))
The draws below stay inside these ranges and needn't reach their ends.
Inputs may be any that keep to these rules, and one draw needn't show every extreme that they name: `page_table`: row o lists the pages of request o of the previous placement, as page numbers of the pool of index o // 2 of req; the rows of one index of req use distinct pages; entries past cached_pages[o] are not part of the cache. A permutation. Either anchor[i] = i, or request i and request anchor[i] lie on two indices of req that differ only in the lowest bit and trade places with each other; an index of req gives and takes at most one request.
All inputs are finite; a program needn't handle non-finite values.
Results may differ from the reference program's by a relative error of at most 0.011.
Values may be sent and summed in bfloat16 or wider, within the bound.
A program may use at most 128 MiB of HBM per device.

```python
import math
import jax
import jax.numpy as jnp
import numpy as np
from jax import lax

MODEL_WIDTH = 1536
QUERY_HEADS = 12
KEY_VALUE_HEADS = 2
HEAD_SIZE = 128
FE = 768
TOPK = 4
NE = 8
REQ_DEV = 2
REQUEST_TOKENS = 512
PAGE_TOKENS = 128
MAXP = 16
REQS = 16
TOK_DEV = 256
NEW_TOKEN_COUNT = 8192
POOL_DEV = 32
TOTAL_PAGES = 256
CAP = 192
N_REQ = 8
N_HEAD = 4


def layout_parts(key):
    key_rows = jax.random.split(jax.random.fold_in(key, 41), 8)
    first_draw = jax.random.randint(key_rows[0], (REQS,), 0, MAXP + 1)
    second_draw = jax.random.randint(key_rows[1], (REQS,), 0, MAXP + 1)
    longest = jax.random.randint(key_rows[2], (), 0, REQS)
    pair_count = REQS // (2 * REQ_DEV)
    trades = jax.random.randint(key_rows[3], (pair_count,), 0, 2).at[0].set(1)
    left_pick = jax.random.randint(key_rows[4], (pair_count,), 0, REQ_DEV)
    right_pick = jax.random.randint(key_rows[5], (pair_count,), 0, REQ_DEV)
    pair_ids = jnp.arange(pair_count, dtype=jnp.int32)
    left_slot = (2 * pair_ids * REQ_DEV + left_pick).astype(jnp.int32)
    right_slot = ((2 * pair_ids + 1) * REQ_DEV + right_pick).astype(jnp.int32)
    cached = (first_draw * second_draw // MAXP).at[longest].set(MAXP)
    cached = cached.at[left_slot[0]].set(MAXP).at[right_slot[0]].set(MAXP).astype(jnp.int32)
    anchor = jnp.arange(REQS, dtype=jnp.int32)
    anchor = anchor.at[left_slot].set(jnp.where(trades == 1, right_slot, left_slot))
    anchor = anchor.at[right_slot].set(jnp.where(trades == 1, left_slot, right_slot))
    device_keys = jax.random.split(key_rows[7], REQS // REQ_DEV)
    table = jax.vmap(lambda one_key: jax.random.permutation(one_key, REQ_DEV * MAXP))(device_keys)
    table = table.reshape(REQS, MAXP).astype(jnp.int32)
    return (cached, anchor, table)


def draw_cached_pages(key, part):
    return layout_parts(key)[0]


def draw_anchor(key, part):
    return layout_parts(key)[1]


def draw_page_table(key, part):
    return layout_parts(key)[2]


def draw_key_page_store(key, part):
    full_shape = (TOTAL_PAGES, PAGE_TOKENS, KEY_VALUE_HEADS * HEAD_SIZE)
    key_rows = jax.random.split(jax.random.fold_in(key, 43), 1)
    drawn = jnp.clip(jax.random.normal(key_rows[0], full_shape, jnp.float32), -6.0, 6.0)
    return drawn.astype(jnp.bfloat16)


def block_levels(key, extent, cuts, low, high):
    def one(dim, shards_of):
        steps = jax.random.uniform(jax.random.fold_in(jax.random.fold_in(key, 6), dim), (shards_of,), jnp.float32, low / len(cuts), high / len(cuts))
        return jnp.repeat(jnp.exp(steps), extent[dim] // shards_of).reshape((-1,) + (1,) * (len(extent) - dim - 1))

    gain = one(*cuts[0])
    for cut in cuts[1:]:
        gain = gain * one(*cut)
    return gain


def routed_block(key, own, number, rows, number_of, top, limit, skew):
    sequence = jax.random.permutation(key, number_of)
    packed, ordinary = load_shares(number_of, rows * top, limit, skew, True), load_shares(number_of, rows * top, limit, skew, False)
    places = jnp.arange(number_of)

    def named(lengths, offset_by):
        used = int((lengths > 0).sum())
        fixed = max(1, used // 4)
        passed = fixed + (places - fixed + offset_by * (used - fixed)) % max(1, number_of - fixed)
        return jnp.zeros((number_of,), jnp.int32).at[sequence[jnp.where(places < fixed, places, passed)]].set(jnp.asarray(lengths, jnp.int32))

    lengths = jnp.where(number % 4 == 0, named(packed, number // 4), named(ordinary, number - number // 4 - 1))
    mixed = jax.random.permutation(jax.random.fold_in(own, 3), number_of)
    giver, taker = mixed[0:number_of // 2 * 2:2], mixed[1:number_of // 2 * 2:2]
    room = jnp.minimum(lengths[giver] - 1, limit - lengths[taker]) // 2
    room = jnp.where((giver == sequence[0]) | (taker == sequence[0]) | (lengths[taker] == 0), 0, jnp.maximum(room, 0))
    passed = jax.random.randint(jax.random.fold_in(own, 4), (number_of // 2,), 0, 1 << 20) % (room + 1)
    lengths = lengths.at[giver].add(-passed).at[taker].add(passed)
    labels = jnp.searchsorted(jnp.cumsum(lengths), jnp.arange(rows * top), side="right").astype(jnp.int32)
    table = labels.reshape(top, rows).T
    table = table[jax.random.permutation(jax.random.fold_in(own, 1), rows)]
    offset_by = jax.random.randint(jax.random.fold_in(own, 2), (rows, 1), 0, top)
    return jnp.take_along_axis(table, (jnp.arange(top)[None, :] + offset_by) % top, axis=1)


def load_shares(number_of, total, most, skew, full):
    loads = [(1 << 20) // math.isqrt(rank ** skew) + 1 for rank in range(1, number_of + 1)]
    largest = most if full else min(most, max(-(-total // number_of), total * loads[0] // sum(loads)))
    least = 1 if total - largest >= number_of - 1 else 0
    given, rest = [largest] + [least] * (number_of - 1), total - largest - least * (number_of - 1)
    while rest > 0:
        free = [i for i in range(1, number_of) if given[i] < largest] or [i for i in range(1, number_of) if given[i] < most]
        whole, remaining = sum([loads[i] for i in free]), rest
        for i in free:
            more = min(most - given[i], max(1, remaining * loads[i] // whole), rest)
            given[i] = given[i] + more
            rest = rest - more
    return np.array(given)


def scatter_about(rng, extent, deviation, limit, shards=(), held_as=jnp.bfloat16):
    array = deviation * jax.random.normal(rng, extent, jnp.float32)
    if shards:
        array = array * block_levels(rng, extent, shards, -0.22, 0.18)
    return jnp.clip(array, -limit, limit).astype(held_as)


def setup_inputs(seed: int = 0) -> dict:
    arg_keys = jax.random.split(jax.random.key(seed), 15)
    tokens = scatter_about(arg_keys[0], (NEW_TOKEN_COUNT, MODEL_WIDTH), 1.0, 6.0, ((0, 32),))
    norm1_gain = jnp.clip(1.0 + 0.18 * jax.random.normal(arg_keys[1], (MODEL_WIDTH,), jnp.float32), 0.1, 1.9)
    query_key_value_weight = scatter_about(arg_keys[2], (MODEL_WIDTH, (QUERY_HEADS + 2 * KEY_VALUE_HEADS) * HEAD_SIZE), MODEL_WIDTH ** -0.5, 0.15625)
    w_out = scatter_about(arg_keys[3], (QUERY_HEADS * HEAD_SIZE, MODEL_WIDTH), (QUERY_HEADS * HEAD_SIZE) ** -0.5, 0.15625)
    norm2_gain = jnp.clip(1.0 + 0.18 * jax.random.normal(arg_keys[4], (MODEL_WIDTH,), jnp.float32), 0.1, 1.9)
    router_weight = scatter_about(arg_keys[5], (MODEL_WIDTH, NE), (4 * MODEL_WIDTH) ** -0.5, 0.078125, (), jnp.float32)
    w_gate_up = scatter_about(arg_keys[6], (NE, MODEL_WIDTH, 2 * FE), MODEL_WIDTH ** -0.5, 0.15625, ((0, 8),))
    w_down = scatter_about(arg_keys[7], (NE, FE, MODEL_WIDTH), FE ** -0.5, 0.21875, ((0, 8),))
    routes_keys = jax.random.split(jax.random.fold_in(arg_keys[8], 1), NEW_TOKEN_COUNT // TOK_DEV)
    routes_turns = jax.random.permutation(jax.random.fold_in(arg_keys[8], 3), NEW_TOKEN_COUNT // TOK_DEV)
    routes = jax.vmap(lambda own, number: routed_block(jax.random.fold_in(arg_keys[8], 2), own, number, TOK_DEV, NE, TOPK, CAP, 2))(routes_keys, routes_turns).reshape((NEW_TOKEN_COUNT, TOPK))
    key_page_store = draw_key_page_store(jax.random.fold_in(arg_keys[14], 71), 0)
    value_page_store = scatter_about(arg_keys[10], (TOTAL_PAGES, PAGE_TOKENS, KEY_VALUE_HEADS * HEAD_SIZE), 1.0, 6.0, ((0, 8),))
    page_table = draw_page_table(jax.random.fold_in(arg_keys[14], 71), 0)
    cached_pages = draw_cached_pages(jax.random.fold_in(arg_keys[14], 71), 0)
    anchor = draw_anchor(jax.random.fold_in(arg_keys[14], 71), 0)
    return {"tokens": tokens, "norm1_gain": norm1_gain, "query_key_value_weight": query_key_value_weight, "w_out": w_out, "norm2_gain": norm2_gain, "router_weight": router_weight, "w_gate_up": w_gate_up, "w_down": w_down, "routes": routes, "key_page_store": key_page_store, "value_page_store": value_page_store, "page_table": page_table, "cached_pages": cached_pages, "anchor": anchor}


EPS = 1e-06
THETA = 1000000.0

def rms_scale(values, gain_vector):
    mean_sq = lax.optimization_barrier(jnp.mean(values * values, axis=-1, keepdims=True))
    return values * lax.rsqrt(mean_sq + EPS) * gain_vector

def apply_rotary(values, where_at):
    half_dim = values.shape[-1] // 2
    frequency = jnp.exp(-jnp.log(jnp.float32(THETA)) * jnp.arange(half_dim, dtype=jnp.float32) * 2.0 / values.shape[-1])
    angles = where_at.astype(jnp.float32)[:, None] * frequency[None, :]
    cosine = jnp.cos(angles)[:, None, :]
    sines = jnp.sin(angles)[:, None, :]
    first_half = values[..., :half_dim]
    second = values[..., half_dim:]
    return jnp.concatenate([first_half * cosine - second * sines, second * cosine + first_half * sines], axis=-1)

def reference(tokens, norm1_gain, query_key_value_weight, w_out, norm2_gain, router_weight, w_gate_up, w_down, routes, key_page_store, value_page_store, page_table, cached_pages, anchor):
    row_ids = jnp.arange(NEW_TOKEN_COUNT, dtype=jnp.int32)
    request_of = row_ids // REQUEST_TOKENS
    token_positions = cached_pages[anchor[request_of]] * PAGE_TOKENS + row_ids % REQUEST_TOKENS
    normed = rms_scale(tokens.astype(jnp.float32), norm1_gain).astype(jnp.bfloat16)
    projected_rows = jnp.dot(normed, query_key_value_weight, preferred_element_type=jnp.float32)
    q_all = apply_rotary(projected_rows[:, :QUERY_HEADS * HEAD_SIZE].reshape(NEW_TOKEN_COUNT, QUERY_HEADS, HEAD_SIZE), token_positions).astype(jnp.bfloat16)
    every_key = apply_rotary(projected_rows[:, QUERY_HEADS * HEAD_SIZE:(QUERY_HEADS + KEY_VALUE_HEADS) * HEAD_SIZE].reshape(NEW_TOKEN_COUNT, KEY_VALUE_HEADS, HEAD_SIZE), token_positions).astype(jnp.bfloat16)
    every_value = projected_rows[:, (QUERY_HEADS + KEY_VALUE_HEADS) * HEAD_SIZE:].astype(jnp.bfloat16)
    appended = jnp.concatenate([every_key.reshape(NEW_TOKEN_COUNT, KEY_VALUE_HEADS * HEAD_SIZE), every_value], axis=1)
    value_heads = every_value.reshape(NEW_TOKEN_COUNT, KEY_VALUE_HEADS, HEAD_SIZE)
    cache_length = MAXP * PAGE_TOKENS
    group_width = QUERY_HEADS // KEY_VALUE_HEADS

    def one_request(request_id):
        old_id = anchor[request_id]
        cached_len = cached_pages[old_id] * PAGE_TOKENS
        page_numbers = old_id // REQ_DEV * POOL_DEV + page_table[old_id]
        cached_key_rows = key_page_store[page_numbers].reshape(cache_length, KEY_VALUE_HEADS, HEAD_SIZE)
        cached_value_rows = value_page_store[page_numbers].reshape(cache_length, KEY_VALUE_HEADS, HEAD_SIZE)
        start_row = (request_id * REQUEST_TOKENS).astype(jnp.int32)
        fresh_queries = lax.dynamic_slice_in_dim(q_all, start_row, REQUEST_TOKENS, 0)
        new_keys = lax.dynamic_slice_in_dim(every_key, start_row, REQUEST_TOKENS, 0)
        new_values = lax.dynamic_slice_in_dim(value_heads, start_row, REQUEST_TOKENS, 0)
        all_keys = jnp.concatenate([cached_key_rows, new_keys], axis=0).astype(jnp.float32)
        all_values = jnp.concatenate([cached_value_rows, new_values], axis=0).astype(jnp.float32)
        key_ids = jnp.arange(cache_length + REQUEST_TOKENS, dtype=jnp.int32)
        span_pos = jnp.arange(REQUEST_TOKENS, dtype=jnp.int32)
        visible = jnp.where(key_ids[None, :] < cache_length, key_ids[None, :] < cached_len, key_ids[None, :] - cache_length <= span_pos[:, None])
        grouped_queries = fresh_queries.astype(jnp.float32).reshape(REQUEST_TOKENS, KEY_VALUE_HEADS, group_width, HEAD_SIZE)
        scores = jnp.einsum('tkgd,ckd->kgtc', grouped_queries, all_keys) * HEAD_SIZE ** (-0.5)
        scores = jnp.where(visible[None, None, :, :], scores, -jnp.inf)
        row_max = lax.optimization_barrier(jnp.max(scores, axis=-1, keepdims=True))
        weights = jnp.exp(scores - row_max)
        row_sums = lax.optimization_barrier(jnp.sum(weights, axis=-1))
        rounded = lax.optimization_barrier(weights.astype(jnp.bfloat16)).astype(jnp.float32)
        summed = jnp.einsum('kgtc,ckd->tkgd', rounded, all_values)
        result = summed / jnp.transpose(row_sums, (2, 0, 1))[..., None]
        return result.reshape(REQUEST_TOKENS, QUERY_HEADS * HEAD_SIZE).astype(jnp.bfloat16)
    attention = lax.map(one_request, jnp.arange(REQS, dtype=jnp.int32)).reshape(NEW_TOKEN_COUNT, QUERY_HEADS * HEAD_SIZE)
    residual = tokens.astype(jnp.float32) + jnp.dot(attention, w_out, preferred_element_type=jnp.float32)
    normed_moe = rms_scale(residual, norm2_gain).astype(jnp.bfloat16)
    logits = jnp.dot(normed_moe.astype(jnp.float32), router_weight, precision=lax.Precision.HIGHEST)
    chosen = jnp.take_along_axis(logits, routes, axis=1)
    sigmoids = jax.nn.sigmoid(chosen)
    route_gates = sigmoids / lax.optimization_barrier(jnp.sum(sigmoids, axis=1, keepdims=True))
    flat_ids = routes.reshape(-1)
    flat_gates = route_gates.reshape(-1)
    sorted_rows = jnp.argsort(flat_ids, stable=True).astype(jnp.int32)
    counts = lax.optimization_barrier(jnp.sum((flat_ids[None, :] == jnp.arange(NE, dtype=jnp.int32)[:, None]).astype(jnp.int32), axis=1))
    starts = (jnp.cumsum(counts) - counts).astype(jnp.int32)
    cap_total = CAP * N_REQ * N_HEAD
    padded_rows = jnp.concatenate([sorted_rows, jnp.zeros((cap_total,), jnp.int32)])

    def expert_step(accumulated, expert_id):
        picked_rows = lax.dynamic_slice_in_dim(padded_rows, starts[expert_id], cap_total, 0)
        valid = jnp.arange(cap_total, dtype=jnp.int32) < counts[expert_id]
        token_ids = picked_rows // TOPK
        inputs = normed_moe[token_ids]
        gate_up = jnp.dot(inputs, w_gate_up[expert_id], preferred_element_type=jnp.float32)
        hidden = (jax.nn.relu(gate_up[:, :FE]) * gate_up[:, FE:]).astype(jnp.bfloat16)
        outputs = jnp.dot(hidden, w_down[expert_id], preferred_element_type=jnp.float32).astype(jnp.bfloat16)
        contrib = jnp.where(valid[:, None], flat_gates[picked_rows][:, None] * outputs.astype(jnp.float32), 0.0)
        return (accumulated.at[token_ids].add(contrib), None)
    expert_sum, _ = lax.scan(expert_step, jnp.zeros((NEW_TOKEN_COUNT, MODEL_WIDTH), jnp.float32), jnp.arange(NE, dtype=jnp.int32))
    mixed = (residual + expert_sum).astype(jnp.bfloat16)
    return (mixed, appended)
```

```python
import functools

import jax
import jax.numpy as jnp
from jax import lax
from jax.experimental import pallas as pl
from jax.experimental.pallas import tpu as pltpu
from jax.sharding import PartitionSpec as P

MODEL_WIDTH = 1536
QUERY_HEADS = 12
KEY_VALUE_HEADS = 2
HEAD_SIZE = 128
FE = 768
TOPK = 4
REQUEST_TOKENS = 512
LANES = 128
HALF = 64

EPS = 1e-06
THETA = 1000000.0
LOG2E = 1.4426950408889634
VMEM_LIMIT = 56 * 1024 * 1024
F32 = jnp.float32
BF16 = jnp.bfloat16


def swapped(value, axis, bit):
    mask = 2**bit
    pairs = [(source, source ^ mask) for source in range(lax.axis_size(axis))]
    return lax.ppermute(value, axis, pairs)


def params(*semantics):
    return pltpu.CompilerParams(
        vmem_limit_bytes=VMEM_LIMIT, dimension_semantics=("arbitrary",) * len(semantics)
    )


def project_kernel(n_groups, x_ref, gain_ref, w_ref, cos_ref, sin_ref, out_ref, app_ref, normed):
    step = pl.program_id(0)
    group_heads = QUERY_HEADS // n_groups
    share = n_groups // KEY_VALUE_HEADS
    width_q = group_heads * HEAD_SIZE

    @pl.when(step == 0)
    def _():
        x = x_ref[...].astype(F32)
        mean_sq = jnp.mean(x * x, axis=-1, keepdims=True)
        normed[...] = (x * lax.rsqrt(mean_sq + EPS) * gain_ref[...]).astype(BF16)

    rows = jnp.dot(normed[...], w_ref[...], preferred_element_type=F32)
    for at in range((QUERY_HEADS + 2 * KEY_VALUE_HEADS) // 2):

        @pl.when(step == at)
        def _(at=at):
            for part in range(2):
                head = 2 * at + part
                value = rows[:, part * HEAD_SIZE : (part + 1) * HEAD_SIZE]
                if head < QUERY_HEADS + KEY_VALUE_HEADS:
                    value = value * cos_ref[...] + pltpu.roll(value, HALF, 1) * sin_ref[...]
                value = value.astype(BF16)
                if head < QUERY_HEADS:
                    low = (head % group_heads) * HEAD_SIZE
                    out_ref[head // group_heads, :, low : low + HEAD_SIZE] = value
                else:
                    kind, kv = divmod(head - QUERY_HEADS, KEY_VALUE_HEADS)
                    low = width_q + kind * HEAD_SIZE
                    for group in range(kv * share, (kv + 1) * share):
                        out_ref[group, :, low : low + HEAD_SIZE] = value
                    low = (head - QUERY_HEADS) * HEAD_SIZE
                    app_ref[:, low : low + HEAD_SIZE] = value


def project(tokens, gain, weight, cosines, sines, n_groups):
    rows = tokens.shape[0]
    row_width = QUERY_HEADS // n_groups * HEAD_SIZE + 2 * HEAD_SIZE
    columns = weight.shape[1]
    tile = 2 * HEAD_SIZE
    whole = lambda *shape: pl.BlockSpec(shape, lambda j: (0,) * len(shape))
    return pl.pallas_call(
        functools.partial(project_kernel, n_groups),
        grid=(columns // tile,),
        in_specs=[
            whole(rows, MODEL_WIDTH),
            whole(1, MODEL_WIDTH),
            pl.BlockSpec((MODEL_WIDTH, tile), lambda j: (0, j)),
            whole(rows, LANES),
            whole(rows, LANES),
        ],
        out_specs=[
            whole(n_groups, rows, row_width),
            whole(rows, 2 * KEY_VALUE_HEADS * HEAD_SIZE),
        ],
        out_shape=[
            jax.ShapeDtypeStruct((n_groups, rows, row_width), BF16),
            jax.ShapeDtypeStruct((rows, 2 * KEY_VALUE_HEADS * HEAD_SIZE), BF16),
        ],
        scratch_shapes=[pltpu.VMEM((rows, MODEL_WIDTH), BF16)],
        compiler_params=params(0),
        cost_estimate=pl.CostEstimate(
            flops=2 * rows * MODEL_WIDTH * columns,
            bytes_accessed=2 * MODEL_WIDTH * columns,
            transcendentals=0,
        ),
        name="project",
    )(tokens, gain.reshape(1, -1), weight, cosines, sines)


def leave_kernel(pages_ref, k_ref, v_ref, out_ref, sems):
    count = out_ref.shape[1]
    column = pl.multiple_of(pages_ref[count] * HEAD_SIZE, HEAD_SIZE)
    copies = []
    for kind, pool in enumerate((k_ref, v_ref)):
        for at in range(count):
            copies.append(
                pltpu.make_async_copy(
                    pool.at[pages_ref[at], :, pl.ds(column, HEAD_SIZE)],
                    out_ref.at[kind, at],
                    sems.at[kind, at],
                )
            )
    for copy in copies:
        copy.start()
    for copy in copies:
        copy.wait()


def leaving_pages(pages, kv_index, k_store, v_store):
    count, page_size = pages.shape[0], k_store.shape[1]
    any_spec = pl.BlockSpec(memory_space=pl.ANY)
    return pl.pallas_call(
        leave_kernel,
        grid_spec=pltpu.PrefetchScalarGridSpec(
            num_scalar_prefetch=1,
            grid=(1,),
            in_specs=[any_spec, any_spec],
            out_specs=any_spec,
            scratch_shapes=[pltpu.SemaphoreType.DMA((2, count))],
        ),
        out_shape=jax.ShapeDtypeStruct((2, count, page_size, HEAD_SIZE), BF16),
        compiler_params=params(0),
        cost_estimate=pl.CostEstimate(
            flops=0, bytes_accessed=8 * count * page_size * HEAD_SIZE, transcendentals=0
        ),
        name="leaving",
    )(jnp.concatenate([pages, kv_index[None]]), k_store, v_store)


def attend_kernel(
    pages_ref, info_ref, rows_ref, k_ref, v_ref, got_ref, out_ref, kbuf, vbuf, top, total, acc, sems
):
    slot = pl.program_id(0)
    n_slots, span, _ = kbuf.shape
    page_size = k_ref.shape[1]
    group_heads = acc.shape[0]
    factor = HEAD_SIZE ** (-0.5) * LOG2E
    column = pl.multiple_of(info_ref[2 * n_slots] * HEAD_SIZE, HEAD_SIZE)
    width_q = group_heads * HEAD_SIZE

    def both(which, page, own):
        place = pl.ds(pl.multiple_of(page * page_size, page_size), page_size)
        pair = []
        for kind, (pool, buf) in enumerate(((k_ref, kbuf), (v_ref, vbuf))):
            if own:
                source = pool.at[pages_ref[which, page], :, pl.ds(column, HEAD_SIZE)]
            else:
                source = got_ref.at[kind, page]
            pair.append(
                pltpu.make_async_copy(source, buf.at[which, place, :], sems.at[which, page, kind])
            )
        return pair

    @pl.when(slot == 0)
    def _():
        for which in range(n_slots):

            @pl.when(info_ref[n_slots + which] == 0)
            def _(which=which):
                @pl.loop(0, info_ref[which])
                def _(page):
                    for copy in both(which, page, True):
                        copy.start()

            @pl.when(info_ref[n_slots + which] != 0)
            def _(which=which):
                @pl.loop(0, info_ref[which])
                def _(page):
                    for copy in both(which, page, False):
                        copy.start()

    keys_t = (((1,), (1,)), ((), ()))
    values_t = (((0,), (0,)), ((), ()))

    def query(head):
        return rows_ref[0, :, head * HEAD_SIZE : (head + 1) * HEAD_SIZE]

    fresh_k = rows_ref[0, :, width_q : width_q + HEAD_SIZE]
    fresh_v = rows_ref[0, :, width_q + HEAD_SIZE : width_q + 2 * HEAD_SIZE]
    tokens = rows_ref.shape[1]
    key_pos = lax.broadcasted_iota(jnp.int32, (tokens, tokens), 0)
    query_pos = lax.broadcasted_iota(jnp.int32, (tokens, tokens), 1)
    for head in range(group_heads):
        scores = lax.dot_general(fresh_k, query(head), keys_t, preferred_element_type=F32)
        scores = jnp.where(key_pos <= query_pos, scores, -jnp.inf)
        largest = jnp.max(scores, axis=0, keepdims=True)
        weights = jnp.exp2((scores - largest) * factor)
        top[head] = largest
        total[head] = jnp.sum(weights, axis=0, keepdims=True)
        acc[head] = lax.dot_general(
            fresh_v, weights.astype(BF16), values_t, preferred_element_type=F32
        )

    def visit(first_page, n_pages):
        for step in range(n_pages):
            for copy in both(slot, first_page + step, True):
                copy.wait()
        place = pl.ds(pl.multiple_of(first_page * page_size, page_size), n_pages * page_size)
        keys = kbuf[slot, place, :]
        values = vbuf[slot, place, :]
        for head in range(group_heads):
            scores = lax.dot_general(keys, query(head), keys_t, preferred_element_type=F32)
            old = top[head]
            largest = jnp.maximum(old, jnp.max(scores, axis=0, keepdims=True))
            fade = jnp.exp2((old - largest) * factor)
            weights = jnp.exp2((scores - largest) * factor)
            top[head] = largest
            total[head] = total[head] * fade + jnp.sum(weights, axis=0, keepdims=True)
            acc[head] = acc[head] * fade + lax.dot_general(
                values, weights.astype(BF16), values_t, preferred_element_type=F32
            )

    count = info_ref[slot]
    full = count // 4

    @pl.loop(0, full)
    def _(at):
        visit(at * 4, 4)

    @pl.loop(full * 4, count)
    def _(page):
        visit(page, 1)

    for head in range(group_heads):
        result = acc[head] / total[head]
        out_ref[0, :, head * HEAD_SIZE : (head + 1) * HEAD_SIZE] = result.T.astype(BF16)


def attend(pages, info, rows, k_store, v_store, got, group_heads):
    n_slots, maxp = pages.shape
    page_size = k_store.shape[1]
    span = maxp * page_size
    width = rows.shape[2]
    width_q = group_heads * HEAD_SIZE
    any_spec = pl.BlockSpec(memory_space=pl.ANY)
    return pl.pallas_call(
        attend_kernel,
        grid_spec=pltpu.PrefetchScalarGridSpec(
            num_scalar_prefetch=2,
            grid=(n_slots,),
            in_specs=[
                pl.BlockSpec((1, REQUEST_TOKENS, width), lambda s, *_: (s, 0, 0)),
                any_spec,
                any_spec,
                any_spec,
            ],
            out_specs=pl.BlockSpec((1, REQUEST_TOKENS, width_q), lambda s, *_: (s, 0, 0)),
            scratch_shapes=[
                pltpu.VMEM((n_slots, span, HEAD_SIZE), BF16),
                pltpu.VMEM((n_slots, span, HEAD_SIZE), BF16),
                pltpu.VMEM((group_heads, 1, REQUEST_TOKENS), F32),
                pltpu.VMEM((group_heads, 1, REQUEST_TOKENS), F32),
                pltpu.VMEM((group_heads, HEAD_SIZE, REQUEST_TOKENS), F32),
                pltpu.SemaphoreType.DMA((n_slots, maxp, 2)),
            ],
        ),
        out_shape=jax.ShapeDtypeStruct((n_slots, REQUEST_TOKENS, width_q), BF16),
        compiler_params=params(0),
        cost_estimate=pl.CostEstimate(
            flops=4 * n_slots * span * REQUEST_TOKENS * width_q,
            bytes_accessed=8 * n_slots * span * HEAD_SIZE,
            transcendentals=n_slots * span * REQUEST_TOKENS * group_heads,
        ),
        name="attend",
    )(pages, info, rows, k_store, v_store, got)


def settle_kernel(x_ref, back_ref, w_ref, gain_ref, router_ref, routes_ref, res_ref, out_ref):
    step = pl.program_id(0)
    product = jnp.dot(back_ref[0], w_ref[...], preferred_element_type=F32)

    @pl.when(step == 0)
    def _():
        res_ref[...] = x_ref[...].astype(F32) + product

    @pl.when(step > 0)
    def _():
        res_ref[...] += product

    @pl.when(step == pl.num_programs(0) - 1)
    def _():
        residual = res_ref[...]
        mean_sq = jnp.mean(residual * residual, axis=-1, keepdims=True)
        normed = (residual * lax.rsqrt(mean_sq + EPS) * gain_ref[...]).astype(BF16)
        out_ref[:, :MODEL_WIDTH] = normed
        logits = jnp.dot(
            normed.astype(F32),
            router_ref[...],
            precision=lax.Precision.HIGHEST,
            preferred_element_type=F32,
        )
        lane = lax.broadcasted_iota(jnp.int32, logits.shape, 1)
        named = lane == routes_ref[:, 0:1]
        for route in range(1, TOPK):
            named = named | (lane == routes_ref[:, route : route + 1])
        sigmoids = jnp.where(named, jax.nn.sigmoid(logits), 0.0)
        gates = sigmoids / jnp.sum(sigmoids, axis=1, keepdims=True)
        high = gates.astype(BF16).astype(F32)
        low = pltpu.roll(gates - high, HALF, 1)
        out_ref[:, MODEL_WIDTH:] = jnp.where(lane < HALF, high, low).astype(BF16)


def settle(tokens, back, w_out, gain, router, routes):
    rows = tokens.shape[0]
    n_groups, _, width_q = back.shape
    whole = lambda *shape: pl.BlockSpec(shape, lambda j: (0,) * len(shape))
    return pl.pallas_call(
        settle_kernel,
        grid=(n_groups,),
        in_specs=[
            whole(rows, MODEL_WIDTH),
            pl.BlockSpec((1, rows, width_q), lambda j: (j, 0, 0)),
            pl.BlockSpec((width_q, MODEL_WIDTH), lambda j: (j, 0)),
            whole(1, MODEL_WIDTH),
            whole(MODEL_WIDTH, LANES),
            whole(rows, TOPK),
        ],
        out_specs=[whole(rows, MODEL_WIDTH), whole(rows, MODEL_WIDTH + LANES)],
        out_shape=[
            jax.ShapeDtypeStruct((rows, MODEL_WIDTH), F32),
            jax.ShapeDtypeStruct((rows, MODEL_WIDTH + LANES), BF16),
        ],
        compiler_params=params(0),
        cost_estimate=pl.CostEstimate(
            flops=2 * rows * MODEL_WIDTH * MODEL_WIDTH,
            bytes_accessed=2 * MODEL_WIDTH * MODEL_WIDTH,
            transcendentals=0,
        ),
        name="settle",
    )(tokens, back, w_out, gain.reshape(1, -1), router, routes)


def expert_kernel(
    ids_ref, xa_ref, xb_ref, gate0, up0, down0, gate1, up1, down1, ya_ref, yb_ref, x, acc, mix
):
    which, part = pl.program_id(1), pl.program_id(2)
    half = xa_ref.shape[0]

    @pl.when((which == 0) & (part == 0))
    def _():
        x[:half] = xa_ref[...]
        x[half:] = xb_ref[...]

    def run(gate_w, up_w, down_w):
        rows = x[:, :MODEL_WIDTH]
        gate = jnp.dot(rows, gate_w[...], preferred_element_type=F32)
        up = jnp.dot(rows, up_w[...], preferred_element_type=F32)
        hidden = (jnp.maximum(gate, 0.0) * up).astype(BF16)
        product = jnp.dot(hidden, down_w[...], preferred_element_type=F32)

        @pl.when(part == 0)
        def _():
            acc[...] = product

        @pl.when(part > 0)
        def _():
            acc[...] += product

    @pl.when(which == 0)
    def _():
        run(gate0, up0, down0)

    @pl.when(which == 1)
    def _():
        run(gate1, up1, down1)

    @pl.when(part == pl.num_programs(2) - 1)
    def _():
        expert = ids_ref[which]
        extra = x[:, MODEL_WIDTH:].astype(F32)
        lane = lax.broadcasted_iota(jnp.int32, extra.shape, 1)
        mine = (lane == expert) | (lane == expert + HALF)
        gate = jnp.sum(jnp.where(mine, extra, 0.0), axis=1, keepdims=True)
        share = acc[...].astype(BF16).astype(F32) * gate

        @pl.when(which == 0)
        def _():
            mix[...] = share

        @pl.when(which == 1)
        def _():
            done = (mix[...] + share).astype(BF16)
            ya_ref[...] = done[:half]
            yb_ref[...] = done[half:]


def experts(ids, xa, xb, weights):
    half_rows, width = xa.shape
    half = min(half_rows, 256)
    tile = 256
    parts = FE // tile
    specs = []
    for which in range(2):
        at = (lambda e, f: jnp.where(e == 0, f, parts - 1)) if which == 0 else (
            lambda e, f: jnp.where(e == 0, 0, f)
        )
        specs += [
            pl.BlockSpec((MODEL_WIDTH, tile), lambda r, e, f, *_, at=at: (0, at(e, f))),
            pl.BlockSpec((MODEL_WIDTH, tile), lambda r, e, f, *_, at=at: (0, parts + at(e, f))),
            pl.BlockSpec((tile, MODEL_WIDTH), lambda r, e, f, *_, at=at: (at(e, f), 0)),
        ]
    row_spec = pl.BlockSpec((half, width), lambda r, e, f, *_: (r, 0))
    out_spec = pl.BlockSpec((half, MODEL_WIDTH), lambda r, e, f, *_: (r, 0))
    operands = []
    for gate_up, down in weights:
        operands += [gate_up, gate_up, down]
    return pl.pallas_call(
        expert_kernel,
        grid_spec=pltpu.PrefetchScalarGridSpec(
            num_scalar_prefetch=1,
            grid=(half_rows // half, 2, parts),
            in_specs=[row_spec, row_spec] + specs,
            out_specs=[out_spec, out_spec],
            scratch_shapes=[
                pltpu.VMEM((2 * half, width), BF16),
                pltpu.VMEM((2 * half, MODEL_WIDTH), F32),
                pltpu.VMEM((2 * half, MODEL_WIDTH), F32),
            ],
        ),
        out_shape=[jax.ShapeDtypeStruct((half_rows, MODEL_WIDTH), BF16)] * 2,
        compiler_params=params(0, 0, 0),
        cost_estimate=pl.CostEstimate(
            flops=24 * half_rows * MODEL_WIDTH * FE,
            bytes_accessed=12 * MODEL_WIDTH * FE,
            transcendentals=0,
        ),
        name="experts",
    )(ids, xa, xb, *operands)


def mixture(ids, sent, weights, n_bits):
    half = sent.shape[0] // 2
    orders = (list(range(n_bits)), list(reversed(range(n_bits))))
    held = [[sent[:half]], [sent[half:]]]
    arrived = []
    for level in range(n_bits):
        pair = []
        for side in range(2):
            buffers = held[side]
            block = buffers[0] if len(buffers) == 1 else jnp.concatenate(buffers, axis=0)
            pair.append(swapped(block, "req", orders[side][level]))
        for side in range(2):
            held[side].append(pair[side])
        arrived.append(pair)
    own = experts(ids, held[0][0], held[1][0], weights)
    outcome = [experts(ids, pair[0], pair[1], weights) for pair in arrived]
    totals = []
    for side in range(2):
        added = [own[side].astype(F32)]
        waiting = [outcome[level][side].astype(F32) for level in range(n_bits)]
        for level in reversed(range(n_bits)):
            back = swapped(waiting[level].astype(BF16), "req", orders[side][level]).astype(F32)
            added.append(back[:half])
            low = half
            for below in range(level):
                size = half * 2**below
                waiting[below] = waiting[below] + back[low : low + size]
                low += size
        totals.append(functools.reduce(jnp.add, added))
    return jnp.concatenate(totals, axis=0)


def on_device(
    tokens,
    norm1_gain,
    query_key_value_weight,
    w_out,
    norm2_gain,
    router_weight,
    w_gate_up,
    w_down,
    routes,
    key_page_store,
    value_page_store,
    page_table,
    cached_pages,
    anchor,
):
    req_index = lax.axis_index("req")
    head_index = lax.axis_index("head")
    n_groups = lax.axis_size("head")
    req_count = lax.axis_size("req")
    rows = tokens.shape[0]
    req_dev = page_table.shape[0]
    page_size = key_page_store.shape[1]
    group_heads = QUERY_HEADS // n_groups
    kv_index = head_index // (n_groups // KEY_VALUE_HEADS)
    far_bit = req_count.bit_length() - 2
    far_mask = 2**far_bit

    partner = req_index ^ 1
    partner_anchor = lax.dynamic_slice_in_dim(anchor, partner * req_dev, req_dev, 0)
    leaving = partner_anchor // req_dev == req_index
    out_row = jnp.sum(jnp.where(leaving, partner_anchor, 0)) % req_dev
    out_pages = lax.dynamic_index_in_dim(page_table, out_row, 0, keepdims=False)
    got = swapped(leaving_pages(out_pages, kv_index, key_page_store, value_page_store), "req", 0)

    gate_rows = w_gate_up.shape[1] // n_groups
    down_rows = w_down.shape[1] // n_groups
    gate_share = lax.dynamic_slice_in_dim(w_gate_up[0], head_index * gate_rows, gate_rows, 0)
    down_share = lax.dynamic_slice_in_dim(w_down[0], head_index * down_rows, down_rows, 0)
    gate_share = swapped(gate_share, "req", far_bit)
    down_share = swapped(down_share, "req", far_bit)
    far_gate_up = lax.all_gather(gate_share, "head", axis=0, tiled=True)
    far_down = lax.all_gather(down_share, "head", axis=0, tiled=True)

    row_ids = (req_index * n_groups + head_index) * rows + jnp.arange(rows, dtype=jnp.int32)
    request = row_ids // REQUEST_TOKENS
    positions = cached_pages[anchor[request]] * page_size + row_ids % REQUEST_TOKENS
    frequency = jnp.exp(
        -jnp.log(F32(THETA)) * jnp.arange(HALF, dtype=F32) * 2.0 / HEAD_SIZE
    )
    angles = positions.astype(F32)[:, None] * frequency[None, :]
    cosine, sine = jnp.cos(angles), jnp.sin(angles)
    outgoing, appended = project(
        tokens,
        norm1_gain,
        query_key_value_weight,
        jnp.concatenate([cosine, cosine], axis=1),
        jnp.concatenate([-sine, sine], axis=1),
        n_groups,
    )
    head_rows = lax.all_to_all(outgoing, "head", split_axis=0, concat_axis=0, tiled=True)
    head_rows = head_rows.reshape(req_dev, REQUEST_TOKENS, outgoing.shape[2])

    slot_anchor = lax.dynamic_slice_in_dim(anchor, req_index * req_dev, req_dev, 0)
    moved = (slot_anchor // req_dev != req_index).astype(jnp.int32)
    pages = page_table[slot_anchor % req_dev]
    info = jnp.concatenate([cached_pages[slot_anchor], moved, kv_index[None].astype(jnp.int32)])
    answers = attend(pages, info, head_rows, key_page_store, value_page_store, got, group_heads)
    answers = answers.reshape(n_groups, rows, group_heads * HEAD_SIZE)
    back = lax.all_to_all(answers, "head", split_axis=0, concat_axis=0, tiled=True)

    router = jnp.pad(router_weight, ((0, 0), (0, LANES - router_weight.shape[1])))
    residual, sent = settle(tokens, back, w_out, norm2_gain, router, routes)
    ids = jnp.stack([req_index, req_index ^ far_mask]).astype(jnp.int32)
    weights = ((w_gate_up[0], w_down[0]), (far_gate_up, far_down))
    mixed = (residual + mixture(ids, sent, weights, far_bit)).astype(BF16)
    return (mixed, appended)


def solution(mesh):
    return jax.shard_map(
        on_device,
        mesh=mesh,
        in_specs=(
            P(("req", "head"), None),
            P(),
            P(),
            P(),
            P(),
            P(),
            P("req", None, None),
            P("req", None, None),
            P(("req", "head"), None),
            P("req", None, None),
            P("req", None, None),
            P("req", None),
            P(),
            P(),
        ),
        out_specs=(P(("req", "head"), None), P(("req", "head"), None)),
        check_vma=False,
    )
```

```python
import functools

import jax
import jax.numpy as jnp
from jax import lax
from jax.experimental import pallas as pl
from jax.experimental.pallas import tpu as pltpu
from jax.sharding import PartitionSpec as P

MODEL_WIDTH = 1536
QUERY_HEADS = 12
KEY_VALUE_HEADS = 2
HEAD_SIZE = 128
FE = 768
TOPK = 4
REQUEST_TOKENS = 512
LANES = 128
HALF = 64

EPS = 1e-06
THETA = 1000000.0
LOG2E = 1.4426950408889634
VMEM_LIMIT = 56 * 1024 * 1024
F32 = jnp.float32
BF16 = jnp.bfloat16


def swapped(value, axis, bit):
    mask = 2**bit
    pairs = [(source, source ^ mask) for source in range(lax.axis_size(axis))]
    return lax.ppermute(value, axis, pairs)


def params(*semantics):
    return pltpu.CompilerParams(
        vmem_limit_bytes=VMEM_LIMIT, dimension_semantics=("arbitrary",) * len(semantics)
    )


def project_kernel(n_groups, x_ref, gain_ref, w_ref, cos_ref, sin_ref, out_ref, app_ref, normed):
    step = pl.program_id(0)
    group_heads = QUERY_HEADS // n_groups
    share = n_groups // KEY_VALUE_HEADS
    width_q = group_heads * HEAD_SIZE

    @pl.when(step == 0)
    def _():
        x = x_ref[...].astype(F32)
        mean_sq = jnp.mean(x * x, axis=-1, keepdims=True)
        normed[...] = (x * lax.rsqrt(mean_sq + EPS) * gain_ref[...]).astype(BF16)

    rows = jnp.dot(normed[...], w_ref[...], preferred_element_type=F32)
    for at in range((QUERY_HEADS + 2 * KEY_VALUE_HEADS) // 2):

        @pl.when(step == at)
        def _(at=at):
            for part in range(2):
                head = 2 * at + part
                value = rows[:, part * HEAD_SIZE : (part + 1) * HEAD_SIZE]
                if head < QUERY_HEADS + KEY_VALUE_HEADS:
                    value = value * cos_ref[...] + pltpu.roll(value, HALF, 1) * sin_ref[...]
                value = value.astype(BF16)
                if head < QUERY_HEADS:
                    low = (head % group_heads) * HEAD_SIZE
                    out_ref[head // group_heads, :, low : low + HEAD_SIZE] = value
                else:
                    kind, kv = divmod(head - QUERY_HEADS, KEY_VALUE_HEADS)
                    low = width_q + kind * HEAD_SIZE
                    for group in range(kv * share, (kv + 1) * share):
                        out_ref[group, :, low : low + HEAD_SIZE] = value
                    low = (head - QUERY_HEADS) * HEAD_SIZE
                    app_ref[:, low : low + HEAD_SIZE] = value


def project(tokens, gain, weight, cosines, sines, n_groups):
    rows = tokens.shape[0]
    row_width = QUERY_HEADS // n_groups * HEAD_SIZE + 2 * HEAD_SIZE
    columns = weight.shape[1]
    tile = 2 * HEAD_SIZE
    whole = lambda *shape: pl.BlockSpec(shape, lambda j: (0,) * len(shape))
    return pl.pallas_call(
        functools.partial(project_kernel, n_groups),
        grid=(columns // tile,),
        in_specs=[
            whole(rows, MODEL_WIDTH),
            whole(1, MODEL_WIDTH),
            pl.BlockSpec((MODEL_WIDTH, tile), lambda j: (0, j)),
            whole(rows, LANES),
            whole(rows, LANES),
        ],
        out_specs=[
            whole(n_groups, rows, row_width),
            whole(rows, 2 * KEY_VALUE_HEADS * HEAD_SIZE),
        ],
        out_shape=[
            jax.ShapeDtypeStruct((n_groups, rows, row_width), BF16),
            jax.ShapeDtypeStruct((rows, 2 * KEY_VALUE_HEADS * HEAD_SIZE), BF16),
        ],
        scratch_shapes=[pltpu.VMEM((rows, MODEL_WIDTH), BF16)],
        compiler_params=params(0),
        cost_estimate=pl.CostEstimate(
            flops=2 * rows * MODEL_WIDTH * columns,
            bytes_accessed=2 * MODEL_WIDTH * columns,
            transcendentals=0,
        ),
        name="project",
    )(tokens, gain.reshape(1, -1), weight, cosines, sines)


def leave_kernel(pages_ref, k_ref, v_ref, out_ref, sems):
    count = out_ref.shape[1]
    column = pl.multiple_of(pages_ref[count] * HEAD_SIZE, HEAD_SIZE)
    copies = []
    for kind, pool in enumerate((k_ref, v_ref)):
        for at in range(count):
            copies.append(
                pltpu.make_async_copy(
                    pool.at[pages_ref[at], :, pl.ds(column, HEAD_SIZE)],
                    out_ref.at[kind, at],
                    sems.at[kind, at],
                )
            )
    for copy in copies:
        copy.start()
    for copy in copies:
        copy.wait()


def leaving_pages(pages, kv_index, k_store, v_store):
    count, page_size = pages.shape[0], k_store.shape[1]
    any_spec = pl.BlockSpec(memory_space=pl.ANY)
    return pl.pallas_call(
        leave_kernel,
        grid_spec=pltpu.PrefetchScalarGridSpec(
            num_scalar_prefetch=1,
            grid=(1,),
            in_specs=[any_spec, any_spec],
            out_specs=pl.BlockSpec(
                (2, count, page_size, HEAD_SIZE), lambda *_: (0, 0, 0, 0)
            ),
            scratch_shapes=[pltpu.SemaphoreType.DMA((2, count))],
        ),
        out_shape=jax.ShapeDtypeStruct((2, count, page_size, HEAD_SIZE), BF16),
        compiler_params=params(0),
        cost_estimate=pl.CostEstimate(
            flops=0, bytes_accessed=8 * count * page_size * HEAD_SIZE, transcendentals=0
        ),
        name="leaving",
    )(jnp.concatenate([pages, kv_index[None]]), k_store, v_store)


def attend_kernel(
    pages_ref, info_ref, rows_ref, k_ref, v_ref, got_ref, more_ref, out_ref, kbuf, vbuf, top, total, acc, sems
):
    slot = pl.program_id(0)
    n_slots, span, _ = kbuf.shape
    page_size = k_ref.shape[1]
    group_heads = acc.shape[0]
    factor = HEAD_SIZE ** (-0.5) * LOG2E
    column = pl.multiple_of(info_ref[2 * n_slots] * HEAD_SIZE, HEAD_SIZE)
    width_q = group_heads * HEAD_SIZE

    fetched = got_ref.shape[1]
    mine = info_ref[2 * n_slots + 1]

    def both(which, page, pool_of=None):
        place = pl.ds(pl.multiple_of(page * page_size, page_size), page_size)
        pair = []
        for kind, (pool, buf) in enumerate(((k_ref, kbuf), (v_ref, vbuf))):
            if pool_of is None:
                source = pool.at[pages_ref[which, page], :, pl.ds(column, HEAD_SIZE)]
            else:
                source = pool_of.at[kind, page % fetched]
            pair.append(
                pltpu.make_async_copy(source, buf.at[which, place, :], sems.at[which, page, kind])
            )
        return pair

    @pl.when(slot == 0)
    def _():
        for which in range(n_slots):

            @pl.when(info_ref[n_slots + which] == 0)
            def _(which=which):
                @pl.loop(0, info_ref[which])
                def _(page):
                    for copy in both(which, page):
                        copy.start()

            @pl.when(info_ref[n_slots + which] != 0)
            def _(which=which):
                @pl.loop(0, info_ref[which])
                def _(page):
                    @pl.when(page // fetched == mine)
                    def _():
                        for copy in both(which, page, got_ref):
                            copy.start()

                    @pl.when(page // fetched != mine)
                    def _():
                        for copy in both(which, page, more_ref):
                            copy.start()

    keys_t = (((1,), (1,)), ((), ()))
    values_t = (((0,), (0,)), ((), ()))

    def query(head):
        return rows_ref[0, :, head * HEAD_SIZE : (head + 1) * HEAD_SIZE]

    fresh_k = rows_ref[0, :, width_q : width_q + HEAD_SIZE]
    fresh_v = rows_ref[0, :, width_q + HEAD_SIZE : width_q + 2 * HEAD_SIZE]
    tokens = rows_ref.shape[1]
    key_pos = lax.broadcasted_iota(jnp.int32, (tokens, tokens), 0)
    query_pos = lax.broadcasted_iota(jnp.int32, (tokens, tokens), 1)
    for head in range(group_heads):
        scores = lax.dot_general(fresh_k, query(head), keys_t, preferred_element_type=F32)
        scores = jnp.where(key_pos <= query_pos, scores, -jnp.inf)
        largest = jnp.max(scores, axis=0, keepdims=True)
        weights = jnp.exp2((scores - largest) * factor)
        top[head] = largest
        total[head] = jnp.sum(weights, axis=0, keepdims=True)
        acc[head] = lax.dot_general(
            fresh_v, weights.astype(BF16), values_t, preferred_element_type=F32
        )

    def visit(first_page, n_pages):
        for step in range(n_pages):
            for copy in both(slot, first_page + step):
                copy.wait()
        place = pl.ds(pl.multiple_of(first_page * page_size, page_size), n_pages * page_size)
        keys = kbuf[slot, place, :]
        values = vbuf[slot, place, :]
        for head in range(group_heads):
            scores = lax.dot_general(keys, query(head), keys_t, preferred_element_type=F32)
            old = top[head]
            largest = jnp.maximum(old, jnp.max(scores, axis=0, keepdims=True))
            fade = jnp.exp2((old - largest) * factor)
            weights = jnp.exp2((scores - largest) * factor)
            top[head] = largest
            total[head] = total[head] * fade + jnp.sum(weights, axis=0, keepdims=True)
            acc[head] = acc[head] * fade + lax.dot_general(
                values, weights.astype(BF16), values_t, preferred_element_type=F32
            )

    count = info_ref[slot]
    full = count // 4

    @pl.loop(0, full)
    def _(at):
        visit(at * 4, 4)

    @pl.loop(full * 4, count)
    def _(page):
        visit(page, 1)

    for head in range(group_heads):
        result = acc[head] / total[head]
        out_ref[0, :, head * HEAD_SIZE : (head + 1) * HEAD_SIZE] = result.T.astype(BF16)


def attend(pages, info, rows, k_store, v_store, got, more, group_heads):
    n_slots, maxp = pages.shape
    page_size = k_store.shape[1]
    span = maxp * page_size
    width = rows.shape[2]
    width_q = group_heads * HEAD_SIZE
    any_spec = pl.BlockSpec(memory_space=pl.ANY)
    return pl.pallas_call(
        attend_kernel,
        grid_spec=pltpu.PrefetchScalarGridSpec(
            num_scalar_prefetch=2,
            grid=(n_slots,),
            in_specs=[
                pl.BlockSpec((1, REQUEST_TOKENS, width), lambda s, *_: (s, 0, 0)),
                any_spec,
                any_spec,
                any_spec,
                any_spec,
            ],
            out_specs=pl.BlockSpec((1, REQUEST_TOKENS, width_q), lambda s, *_: (s, 0, 0)),
            scratch_shapes=[
                pltpu.VMEM((n_slots, span, HEAD_SIZE), BF16),
                pltpu.VMEM((n_slots, span, HEAD_SIZE), BF16),
                pltpu.VMEM((group_heads, 1, REQUEST_TOKENS), F32),
                pltpu.VMEM((group_heads, 1, REQUEST_TOKENS), F32),
                pltpu.VMEM((group_heads, HEAD_SIZE, REQUEST_TOKENS), F32),
                pltpu.SemaphoreType.DMA((n_slots, maxp, 2)),
            ],
        ),
        out_shape=jax.ShapeDtypeStruct((n_slots, REQUEST_TOKENS, width_q), BF16),
        compiler_params=params(0),
        cost_estimate=pl.CostEstimate(
            flops=4 * n_slots * span * REQUEST_TOKENS * width_q,
            bytes_accessed=8 * n_slots * span * HEAD_SIZE,
            transcendentals=n_slots * span * REQUEST_TOKENS * group_heads,
        ),
        name="attend",
    )(pages, info, rows, k_store, v_store, got, more)


def settle_kernel(x_ref, back_ref, w_ref, gain_ref, router_ref, routes_ref, res_ref, out_ref):
    step = pl.program_id(0)
    product = jnp.dot(back_ref[0], w_ref[...], preferred_element_type=F32)

    @pl.when(step == 0)
    def _():
        res_ref[...] = x_ref[...].astype(F32) + product

    @pl.when(step > 0)
    def _():
        res_ref[...] += product

    @pl.when(step == pl.num_programs(0) - 1)
    def _():
        residual = res_ref[...]
        mean_sq = jnp.mean(residual * residual, axis=-1, keepdims=True)
        normed = (residual * lax.rsqrt(mean_sq + EPS) * gain_ref[...]).astype(BF16)
        out_ref[:, :MODEL_WIDTH] = normed
        logits = jnp.dot(
            normed.astype(F32),
            router_ref[...],
            precision=lax.Precision.HIGHEST,
            preferred_element_type=F32,
        )
        lane = lax.broadcasted_iota(jnp.int32, logits.shape, 1)
        named = lane == routes_ref[:, 0:1]
        for route in range(1, TOPK):
            named = named | (lane == routes_ref[:, route : route + 1])
        sigmoids = jnp.where(named, jax.nn.sigmoid(logits), 0.0)
        gates = sigmoids / jnp.sum(sigmoids, axis=1, keepdims=True)
        high = gates.astype(BF16).astype(F32)
        low = pltpu.roll(gates - high, HALF, 1)
        out_ref[:, MODEL_WIDTH:] = jnp.where(lane < HALF, high, low).astype(BF16)


def settle(tokens, back, w_out, gain, router, routes):
    rows = tokens.shape[0]
    n_groups, _, width_q = back.shape
    whole = lambda *shape: pl.BlockSpec(shape, lambda j: (0,) * len(shape))
    return pl.pallas_call(
        settle_kernel,
        grid=(n_groups,),
        in_specs=[
            whole(rows, MODEL_WIDTH),
            pl.BlockSpec((1, rows, width_q), lambda j: (j, 0, 0)),
            pl.BlockSpec((width_q, MODEL_WIDTH), lambda j: (j, 0)),
            whole(1, MODEL_WIDTH),
            whole(MODEL_WIDTH, LANES),
            whole(rows, TOPK),
        ],
        out_specs=[whole(rows, MODEL_WIDTH), whole(rows, MODEL_WIDTH + LANES)],
        out_shape=[
            jax.ShapeDtypeStruct((rows, MODEL_WIDTH), F32),
            jax.ShapeDtypeStruct((rows, MODEL_WIDTH + LANES), BF16),
        ],
        compiler_params=params(0),
        cost_estimate=pl.CostEstimate(
            flops=2 * rows * MODEL_WIDTH * MODEL_WIDTH,
            bytes_accessed=2 * MODEL_WIDTH * MODEL_WIDTH,
            transcendentals=0,
        ),
        name="settle",
    )(tokens, back, w_out, gain.reshape(1, -1), router, routes)


def expert_kernel(
    ids_ref, xa_ref, xb_ref, gate0, up0, down0, gate1, up1, gate2, up2, down1, ya_ref, yb_ref, x, acc, mix
):
    which, part = pl.program_id(1), pl.program_id(2)
    half = xa_ref.shape[0]

    @pl.when((which == 0) & (part == 0))
    def _():
        x[:half] = xa_ref[...]
        x[half:] = xb_ref[...]

    def product_of(pieces):
        total, low = None, 0
        for piece in pieces:
            depth = piece.shape[0]
            term = jnp.dot(x[:, low : low + depth], piece[...], preferred_element_type=F32)
            total = term if total is None else total + term
            low += depth
        return total

    def run(gate_w, up_w, down_w):
        gate = product_of(gate_w)
        up = product_of(up_w)
        hidden = (jnp.maximum(gate, 0.0) * up).astype(BF16)
        product = jnp.dot(hidden, down_w[...], preferred_element_type=F32)

        @pl.when(part == 0)
        def _():
            acc[...] = product

        @pl.when(part > 0)
        def _():
            acc[...] += product

    @pl.when(which == 0)
    def _():
        run((gate0,), (up0,), down0)

    @pl.when(which == 1)
    def _():
        run((gate1, gate2), (up1, up2), down1)

    @pl.when(part == pl.num_programs(2) - 1)
    def _():
        expert = ids_ref[which]
        extra = x[:, MODEL_WIDTH:].astype(F32)
        lane = lax.broadcasted_iota(jnp.int32, extra.shape, 1)
        mine = (lane == expert) | (lane == expert + HALF)
        gate = jnp.sum(jnp.where(mine, extra, 0.0), axis=1, keepdims=True)
        share = acc[...].astype(BF16).astype(F32) * gate

        @pl.when(which == 0)
        def _():
            mix[...] = share

        @pl.when(which == 1)
        def _():
            done = (mix[...] + share).astype(BF16)
            ya_ref[...] = done[:half]
            yb_ref[...] = done[half:]


def experts(ids, xa, xb, weights):
    half_rows, width = xa.shape
    half = min(half_rows, 256)
    tile = 256
    parts = FE // tile
    specs, operands = [], []
    for which, (gate_ups, down) in enumerate(weights):
        if which == 0:
            at = lambda e, f: jnp.where(e == 0, f, parts - 1)
        else:
            at = lambda e, f: jnp.where(e == 0, 0, f)
        for gate_up in gate_ups:
            shape = (gate_up.shape[0], tile)
            specs += [
                pl.BlockSpec(shape, lambda r, e, f, *_, at=at: (0, at(e, f))),
                pl.BlockSpec(shape, lambda r, e, f, *_, at=at: (0, parts + at(e, f))),
            ]
            operands += [gate_up, gate_up]
        specs.append(pl.BlockSpec((tile, MODEL_WIDTH), lambda r, e, f, *_, at=at: (at(e, f), 0)))
        operands.append(down)
    row_spec = pl.BlockSpec((half, width), lambda r, e, f, *_: (r, 0))
    out_spec = pl.BlockSpec((half, MODEL_WIDTH), lambda r, e, f, *_: (r, 0))
    return pl.pallas_call(
        expert_kernel,
        grid_spec=pltpu.PrefetchScalarGridSpec(
            num_scalar_prefetch=1,
            grid=(half_rows // half, 2, parts),
            in_specs=[row_spec, row_spec] + specs,
            out_specs=[out_spec, out_spec],
            scratch_shapes=[
                pltpu.VMEM((2 * half, width), BF16),
                pltpu.VMEM((2 * half, MODEL_WIDTH), F32),
                pltpu.VMEM((2 * half, MODEL_WIDTH), F32),
            ],
        ),
        out_shape=[jax.ShapeDtypeStruct((half_rows, MODEL_WIDTH), BF16)] * 2,
        compiler_params=params(0, 0, 0),
        cost_estimate=pl.CostEstimate(
            flops=24 * half_rows * MODEL_WIDTH * FE,
            bytes_accessed=12 * MODEL_WIDTH * FE,
            transcendentals=0,
        ),
        name="experts",
    )(ids, xa, xb, *operands)


def mixture(ids, sent, weights, n_bits):
    half = sent.shape[0] // 2
    orders = (list(range(n_bits)), list(reversed(range(n_bits))))
    held = [[sent[:half]], [sent[half:]]]
    arrived = []
    for level in range(n_bits):
        pair = []
        for side in range(2):
            buffers = held[side]
            block = buffers[0] if len(buffers) == 1 else jnp.concatenate(buffers, axis=0)
            pair.append(swapped(block, "req", orders[side][level]))
        for side in range(2):
            held[side].append(pair[side])
        arrived.append(pair)
    early = experts(
        ids,
        jnp.concatenate(held[0][:-1], axis=0),
        jnp.concatenate(held[1][:-1], axis=0),
        weights,
    )
    early, last = lax.optimization_barrier((tuple(early), tuple(arrived[-1])))
    late = experts(ids, last[0], last[1], weights)
    totals = []
    for side in range(2):
        added = [early[side][:half].astype(F32)]
        waiting, low = [], half
        for level in range(n_bits - 1):
            size = half * 2**level
            waiting.append(early[side][low : low + size].astype(F32))
            low += size
        waiting.append(late[side].astype(F32))
        for level in reversed(range(n_bits)):
            back = swapped(waiting[level].astype(BF16), "req", orders[side][level]).astype(F32)
            added.append(back[:half])
            low = half
            for below in range(level):
                size = half * 2**below
                waiting[below] = waiting[below] + back[low : low + size]
                low += size
        totals.append(functools.reduce(jnp.add, added))
    return jnp.concatenate(totals, axis=0)


def on_device(
    tokens,
    norm1_gain,
    query_key_value_weight,
    w_out,
    norm2_gain,
    router_weight,
    w_gate_up,
    w_down,
    routes,
    key_page_store,
    value_page_store,
    page_table,
    cached_pages,
    anchor,
):
    req_index = lax.axis_index("req")
    head_index = lax.axis_index("head")
    n_groups = lax.axis_size("head")
    req_count = lax.axis_size("req")
    rows = tokens.shape[0]
    req_dev = page_table.shape[0]
    page_size = key_page_store.shape[1]
    group_heads = QUERY_HEADS // n_groups
    kv_index = head_index // (n_groups // KEY_VALUE_HEADS)
    far_bit = req_count.bit_length() - 2
    far_mask = 2**far_bit

    partner = req_index ^ 1
    partner_anchor = lax.dynamic_slice_in_dim(anchor, partner * req_dev, req_dev, 0)
    leaving = partner_anchor // req_dev == req_index
    out_row = jnp.sum(jnp.where(leaving, partner_anchor, 0)) % req_dev
    out_pages = lax.dynamic_index_in_dim(page_table, out_row, 0, keepdims=False)
    half_pages = page_table.shape[1] // 2
    core = head_index % 2
    out_pages = lax.dynamic_slice_in_dim(out_pages, core * half_pages, half_pages, 0)
    left = leaving_pages(out_pages, kv_index, key_page_store, value_page_store)
    tokens, left = lax.optimization_barrier((tokens, left))
    got = swapped(left, "req", 0)

    def share_of(block):
        count = block.shape[0] // n_groups
        return lax.dynamic_slice_in_dim(block, head_index * count, count, 0)

    middle = w_gate_up.shape[1] // 2
    far_down = swapped(share_of(w_down[0]), "req", far_bit)
    far_first = swapped(share_of(w_gate_up[0, :middle]), "req", far_bit)
    far_second = swapped(share_of(w_gate_up[0, middle:]), "req", far_bit)

    first_row = (req_index * n_groups + head_index) * rows
    start = cached_pages[anchor[first_row // REQUEST_TOKENS]] * page_size
    positions = start + first_row % REQUEST_TOKENS + jnp.arange(rows, dtype=jnp.int32)
    frequency = jnp.exp(
        -jnp.log(F32(THETA)) * jnp.arange(HALF, dtype=F32) * 2.0 / HEAD_SIZE
    )
    angles = positions.astype(F32)[:, None] * frequency[None, :]
    cosine, sine = jnp.cos(angles), jnp.sin(angles)
    outgoing, appended = project(
        tokens,
        norm1_gain,
        query_key_value_weight,
        jnp.concatenate([cosine, cosine], axis=1),
        jnp.concatenate([-sine, sine], axis=1),
        n_groups,
    )
    outgoing, got = lax.optimization_barrier((outgoing, got))
    more = swapped(got, "head", 0)
    head_rows = lax.all_to_all(outgoing, "head", split_axis=0, concat_axis=0, tiled=True)
    head_rows, far_down = lax.optimization_barrier((head_rows, far_down))
    far_down = lax.all_gather(far_down, "head", axis=0, tiled=True)
    head_rows = head_rows.reshape(req_dev, REQUEST_TOKENS, outgoing.shape[2])

    slot_anchor = lax.dynamic_slice_in_dim(anchor, req_index * req_dev, req_dev, 0)
    moved = (slot_anchor // req_dev != req_index).astype(jnp.int32)
    pages = page_table[slot_anchor % req_dev]
    info = jnp.concatenate([cached_pages[slot_anchor], moved, jnp.stack([kv_index, core]).astype(jnp.int32)])
    answers = attend(pages, info, head_rows, key_page_store, value_page_store, got, more, group_heads)
    answers = answers.reshape(n_groups, rows, group_heads * HEAD_SIZE)
    answers, far_first = lax.optimization_barrier((answers, far_first))
    far_first = lax.all_gather(far_first, "head", axis=0, tiled=True)
    back = lax.all_to_all(answers, "head", split_axis=0, concat_axis=0, tiled=True)

    router = jnp.pad(router_weight, ((0, 0), (0, LANES - router_weight.shape[1])))
    residual, sent = settle(tokens, back, w_out, norm2_gain, router, routes)
    sent, far_second = lax.optimization_barrier((sent, far_second))
    far_second = lax.all_gather(far_second, "head", axis=0, tiled=True)
    ids = jnp.stack([req_index, req_index ^ far_mask]).astype(jnp.int32)
    weights = (((w_gate_up[0],), w_down[0]), ((far_first, far_second), far_down))
    mixed = (residual + mixture(ids, sent, weights, far_bit)).astype(BF16)
    return (mixed, appended)


def solution(mesh):
    return jax.shard_map(
        on_device,
        mesh=mesh,
        in_specs=(
            P(("req", "head"), None),
            P(),
            P(),
            P(),
            P(),
            P(),
            P("req", None, None),
            P("req", None, None),
            P(("req", "head"), None),
            P("req", None, None),
            P("req", None, None),
            P("req", None),
            P(),
            P(),
        ),
        out_specs=(P(("req", "head"), None), P(("req", "head"), None)),
        check_vma=False,
    )
```

```python
import functools

import jax
import jax.numpy as jnp
from jax import lax
from jax.experimental import pallas as pl
from jax.experimental.pallas import tpu as pltpu
from jax.sharding import PartitionSpec as P

MODEL_WIDTH = 1536
QUERY_HEADS = 12
KEY_VALUE_HEADS = 2
HEAD_SIZE = 128
FE = 768
TOPK = 4
REQUEST_TOKENS = 512
LANES = 128
HALF = 64

EPS = 1e-06
THETA = 1000000.0
LOG2E = 1.4426950408889634
VMEM_LIMIT = 56 * 1024 * 1024
F32 = jnp.float32
BF16 = jnp.bfloat16


def swapped(value, axis, bit):
    mask = 2**bit
    pairs = [(source, source ^ mask) for source in range(lax.axis_size(axis))]
    return lax.ppermute(value, axis, pairs)


def params(*semantics):
    return pltpu.CompilerParams(
        vmem_limit_bytes=VMEM_LIMIT, dimension_semantics=("arbitrary",) * len(semantics)
    )


def project_kernel(n_groups, x_ref, gain_ref, w_ref, cos_ref, sin_ref, out_ref, app_ref, normed):
    step = pl.program_id(0)
    group_heads = QUERY_HEADS // n_groups
    share = n_groups // KEY_VALUE_HEADS
    width_q = group_heads * HEAD_SIZE

    @pl.when(step == 0)
    def _():
        x = x_ref[...].astype(F32)
        mean_sq = jnp.mean(x * x, axis=-1, keepdims=True)
        normed[...] = (x * lax.rsqrt(mean_sq + EPS) * gain_ref[...]).astype(BF16)

    rows = jnp.dot(normed[...], w_ref[...], preferred_element_type=F32)
    for at in range((QUERY_HEADS + 2 * KEY_VALUE_HEADS) // 2):

        @pl.when(step == at)
        def _(at=at):
            for part in range(2):
                head = 2 * at + part
                value = rows[:, part * HEAD_SIZE : (part + 1) * HEAD_SIZE]
                if head < QUERY_HEADS + KEY_VALUE_HEADS:
                    value = value * cos_ref[...] + pltpu.roll(value, HALF, 1) * sin_ref[...]
                value = value.astype(BF16)
                if head < QUERY_HEADS:
                    low = (head % group_heads) * HEAD_SIZE
                    out_ref[head // group_heads, :, low : low + HEAD_SIZE] = value
                else:
                    kind, kv = divmod(head - QUERY_HEADS, KEY_VALUE_HEADS)
                    low = width_q + kind * HEAD_SIZE
                    for group in range(kv * share, (kv + 1) * share):
                        out_ref[group, :, low : low + HEAD_SIZE] = value
                    low = (head - QUERY_HEADS) * HEAD_SIZE
                    app_ref[:, low : low + HEAD_SIZE] = value


def project(tokens, gain, weight, cosines, sines, n_groups):
    rows = tokens.shape[0]
    row_width = QUERY_HEADS // n_groups * HEAD_SIZE + 2 * HEAD_SIZE
    columns = weight.shape[1]
    tile = 2 * HEAD_SIZE
    whole = lambda *shape: pl.BlockSpec(shape, lambda j: (0,) * len(shape))
    return pl.pallas_call(
        functools.partial(project_kernel, n_groups),
        grid=(columns // tile,),
        in_specs=[
            whole(rows, MODEL_WIDTH),
            whole(1, MODEL_WIDTH),
            pl.BlockSpec((MODEL_WIDTH, tile), lambda j: (0, j)),
            whole(rows, LANES),
            whole(rows, LANES),
        ],
        out_specs=[
            whole(n_groups, rows, row_width),
            whole(rows, 2 * KEY_VALUE_HEADS * HEAD_SIZE),
        ],
        out_shape=[
            jax.ShapeDtypeStruct((n_groups, rows, row_width), BF16),
            jax.ShapeDtypeStruct((rows, 2 * KEY_VALUE_HEADS * HEAD_SIZE), BF16),
        ],
        scratch_shapes=[pltpu.VMEM((rows, MODEL_WIDTH), BF16)],
        compiler_params=params(0),
        cost_estimate=pl.CostEstimate(
            flops=2 * rows * MODEL_WIDTH * columns,
            bytes_accessed=2 * MODEL_WIDTH * columns,
            transcendentals=0,
        ),
        name="project",
    )(tokens, gain.reshape(1, -1), weight, cosines, sines)


def leave_kernel(pages_ref, k_ref, v_ref, out_ref, sems):
    count = out_ref.shape[1]
    column = pl.multiple_of(pages_ref[count] * HEAD_SIZE, HEAD_SIZE)
    copies = []
    for kind, pool in enumerate((k_ref, v_ref)):
        for at in range(count):
            copies.append(
                pltpu.make_async_copy(
                    pool.at[pages_ref[at], :, pl.ds(column, HEAD_SIZE)],
                    out_ref.at[kind, at],
                    sems.at[kind, at],
                )
            )
    for copy in copies:
        copy.start()
    for copy in copies:
        copy.wait()


def leaving_pages(pages, kv_index, k_store, v_store):
    count, page_size = pages.shape[0], k_store.shape[1]
    any_spec = pl.BlockSpec(memory_space=pl.ANY)
    return pl.pallas_call(
        leave_kernel,
        grid_spec=pltpu.PrefetchScalarGridSpec(
            num_scalar_prefetch=1,
            grid=(1,),
            in_specs=[any_spec, any_spec],
            out_specs=pl.BlockSpec(
                (2, count, page_size, HEAD_SIZE), lambda *_: (0, 0, 0, 0)
            ),
            scratch_shapes=[pltpu.SemaphoreType.DMA((2, count))],
        ),
        out_shape=jax.ShapeDtypeStruct((2, count, page_size, HEAD_SIZE), BF16),
        compiler_params=params(0),
        cost_estimate=pl.CostEstimate(
            flops=0, bytes_accessed=8 * count * page_size * HEAD_SIZE, transcendentals=0
        ),
        name="leaving",
    )(jnp.concatenate([pages, kv_index[None]]), k_store, v_store)


def attend_kernel(
    pages_ref, info_ref, rows_ref, k_ref, v_ref, got_ref, more_ref, out_ref, kbuf, vbuf, top, total, acc, sems
):
    slot = pl.program_id(0)
    n_slots, span, _ = kbuf.shape
    page_size = k_ref.shape[1]
    group_heads = acc.shape[0]
    factor = HEAD_SIZE ** (-0.5) * LOG2E
    column = pl.multiple_of(info_ref[2 * n_slots] * HEAD_SIZE, HEAD_SIZE)
    width_q = group_heads * HEAD_SIZE

    fetched = got_ref.shape[1]
    mine = info_ref[2 * n_slots + 1]

    def both(which, page, pool_of=None):
        place = pl.ds(pl.multiple_of(page * page_size, page_size), page_size)
        pair = []
        for kind, (pool, buf) in enumerate(((k_ref, kbuf), (v_ref, vbuf))):
            if pool_of is None:
                source = pool.at[pages_ref[which, page], :, pl.ds(column, HEAD_SIZE)]
            else:
                source = pool_of.at[kind, page % fetched]
            pair.append(
                pltpu.make_async_copy(source, buf.at[which, place, :], sems.at[which, page, kind])
            )
        return pair

    @pl.when(slot == 0)
    def _():
        for which in range(n_slots):

            @pl.when(info_ref[n_slots + which] == 0)
            def _(which=which):
                @pl.loop(0, info_ref[which])
                def _(page):
                    for copy in both(which, page):
                        copy.start()

            @pl.when(info_ref[n_slots + which] != 0)
            def _(which=which):
                @pl.loop(0, info_ref[which])
                def _(page):
                    @pl.when(page // fetched == mine)
                    def _():
                        for copy in both(which, page, got_ref):
                            copy.start()

                    @pl.when(page // fetched != mine)
                    def _():
                        for copy in both(which, page, more_ref):
                            copy.start()

    keys_t = (((1,), (1,)), ((), ()))
    values_t = (((0,), (0,)), ((), ()))

    def query(head):
        return rows_ref[0, :, head * HEAD_SIZE : (head + 1) * HEAD_SIZE]

    fresh_k = rows_ref[0, :, width_q : width_q + HEAD_SIZE]
    fresh_v = rows_ref[0, :, width_q + HEAD_SIZE : width_q + 2 * HEAD_SIZE]
    tokens = rows_ref.shape[1]
    key_pos = lax.broadcasted_iota(jnp.int32, (tokens, tokens), 0)
    query_pos = lax.broadcasted_iota(jnp.int32, (tokens, tokens), 1)
    for head in range(group_heads):
        scores = lax.dot_general(fresh_k, query(head), keys_t, preferred_element_type=F32)
        scores = jnp.where(key_pos <= query_pos, scores, -jnp.inf)
        largest = jnp.max(scores, axis=0, keepdims=True)
        weights = jnp.exp2((scores - largest) * factor)
        top[head] = largest
        total[head] = jnp.sum(weights, axis=0, keepdims=True)
        acc[head] = lax.dot_general(
            fresh_v, weights.astype(BF16), values_t, preferred_element_type=F32
        )

    def visit(first_page, n_pages):
        for step in range(n_pages):
            for copy in both(slot, first_page + step):
                copy.wait()
        place = pl.ds(pl.multiple_of(first_page * page_size, page_size), n_pages * page_size)
        keys = kbuf[slot, place, :]
        values = vbuf[slot, place, :]
        for head in range(group_heads):
            scores = lax.dot_general(keys, query(head), keys_t, preferred_element_type=F32)
            old = top[head]
            largest = jnp.maximum(old, jnp.max(scores, axis=0, keepdims=True))
            fade = jnp.exp2((old - largest) * factor)
            weights = jnp.exp2((scores - largest) * factor)
            top[head] = largest
            total[head] = total[head] * fade + jnp.sum(weights, axis=0, keepdims=True)
            acc[head] = acc[head] * fade + lax.dot_general(
                values, weights.astype(BF16), values_t, preferred_element_type=F32
            )

    count = info_ref[slot]
    full = count // 4

    @pl.loop(0, full)
    def _(at):
        visit(at * 4, 4)

    @pl.loop(full * 4, count)
    def _(page):
        visit(page, 1)

    for head in range(group_heads):
        result = acc[head] / total[head]
        out_ref[0, :, head * HEAD_SIZE : (head + 1) * HEAD_SIZE] = result.T.astype(BF16)


def attend(pages, info, rows, k_store, v_store, got, more, group_heads):
    n_slots, maxp = pages.shape
    page_size = k_store.shape[1]
    span = maxp * page_size
    width = rows.shape[2]
    width_q = group_heads * HEAD_SIZE
    any_spec = pl.BlockSpec(memory_space=pl.ANY)
    return pl.pallas_call(
        attend_kernel,
        grid_spec=pltpu.PrefetchScalarGridSpec(
            num_scalar_prefetch=2,
            grid=(n_slots,),
            in_specs=[
                pl.BlockSpec((1, REQUEST_TOKENS, width), lambda s, *_: (s, 0, 0)),
                any_spec,
                any_spec,
                any_spec,
                any_spec,
            ],
            out_specs=pl.BlockSpec((1, REQUEST_TOKENS, width_q), lambda s, *_: (s, 0, 0)),
            scratch_shapes=[
                pltpu.VMEM((n_slots, span, HEAD_SIZE), BF16),
                pltpu.VMEM((n_slots, span, HEAD_SIZE), BF16),
                pltpu.VMEM((group_heads, 1, REQUEST_TOKENS), F32),
                pltpu.VMEM((group_heads, 1, REQUEST_TOKENS), F32),
                pltpu.VMEM((group_heads, HEAD_SIZE, REQUEST_TOKENS), F32),
                pltpu.SemaphoreType.DMA((n_slots, maxp, 2)),
            ],
        ),
        out_shape=jax.ShapeDtypeStruct((n_slots, REQUEST_TOKENS, width_q), BF16),
        compiler_params=params(0),
        cost_estimate=pl.CostEstimate(
            flops=4 * n_slots * span * REQUEST_TOKENS * width_q,
            bytes_accessed=8 * n_slots * span * HEAD_SIZE,
            transcendentals=n_slots * span * REQUEST_TOKENS * group_heads,
        ),
        name="attend",
    )(pages, info, rows, k_store, v_store, got, more)


def settle_kernel(x_ref, back_ref, w_ref, gain_ref, router_ref, routes_ref, res_ref, out_ref):
    step = pl.program_id(0)
    product = jnp.dot(back_ref[0], w_ref[...], preferred_element_type=F32)

    @pl.when(step == 0)
    def _():
        res_ref[...] = x_ref[...].astype(F32) + product

    @pl.when(step > 0)
    def _():
        res_ref[...] += product

    @pl.when(step == pl.num_programs(0) - 1)
    def _():
        residual = res_ref[...]
        mean_sq = jnp.mean(residual * residual, axis=-1, keepdims=True)
        normed = (residual * lax.rsqrt(mean_sq + EPS) * gain_ref[...]).astype(BF16)
        out_ref[:, :MODEL_WIDTH] = normed
        logits = jnp.dot(
            normed.astype(F32),
            router_ref[...],
            precision=lax.Precision.HIGHEST,
            preferred_element_type=F32,
        )
        lane = lax.broadcasted_iota(jnp.int32, logits.shape, 1)
        named = lane == routes_ref[:, 0:1]
        for route in range(1, TOPK):
            named = named | (lane == routes_ref[:, route : route + 1])
        sigmoids = jnp.where(named, jax.nn.sigmoid(logits), 0.0)
        gates = sigmoids / jnp.sum(sigmoids, axis=1, keepdims=True)
        high = gates.astype(BF16).astype(F32)
        low = pltpu.roll(gates - high, HALF, 1)
        out_ref[:, MODEL_WIDTH:] = jnp.where(lane < HALF, high, low).astype(BF16)


def settle(tokens, back, w_out, gain, router, routes):
    rows = tokens.shape[0]
    n_groups, _, width_q = back.shape
    whole = lambda *shape: pl.BlockSpec(shape, lambda j: (0,) * len(shape))
    return pl.pallas_call(
        settle_kernel,
        grid=(n_groups,),
        in_specs=[
            whole(rows, MODEL_WIDTH),
            pl.BlockSpec((1, rows, width_q), lambda j: (j, 0, 0)),
            pl.BlockSpec((width_q, MODEL_WIDTH), lambda j: (j, 0)),
            whole(1, MODEL_WIDTH),
            whole(MODEL_WIDTH, LANES),
            whole(rows, TOPK),
        ],
        out_specs=[whole(rows, MODEL_WIDTH), whole(rows, MODEL_WIDTH + LANES)],
        out_shape=[
            jax.ShapeDtypeStruct((rows, MODEL_WIDTH), F32),
            jax.ShapeDtypeStruct((rows, MODEL_WIDTH + LANES), BF16),
        ],
        compiler_params=params(0),
        cost_estimate=pl.CostEstimate(
            flops=2 * rows * MODEL_WIDTH * MODEL_WIDTH,
            bytes_accessed=2 * MODEL_WIDTH * MODEL_WIDTH,
            transcendentals=0,
        ),
        name="settle",
    )(tokens, back, w_out, gain.reshape(1, -1), router, routes)


def expert_kernel(layout, ids_ref, xa_ref, xb_ref, *refs):
    ya_ref, yb_ref, x, acc, mix = refs[-5:]
    which, part = pl.program_id(1), pl.program_id(2)
    half = xa_ref.shape[0]

    @pl.when((which == 0) & (part == 0))
    def _():
        x[:half] = xa_ref[...]
        x[half:] = xb_ref[...]

    def product_of(pieces):
        total, low = None, 0
        for piece in pieces:
            depth = piece.shape[0]
            term = jnp.dot(x[:, low : low + depth], piece[...], preferred_element_type=F32)
            total = term if total is None else total + term
            low += depth
        return total

    def run(gate_w, up_w, down_w):
        gate = product_of(gate_w)
        up = product_of(up_w)
        hidden = (jnp.maximum(gate, 0.0) * up).astype(BF16)
        product = jnp.dot(hidden, down_w[...], preferred_element_type=F32)

        @pl.when(part == 0)
        def _():
            acc[...] = product

        @pl.when(part > 0)
        def _():
            acc[...] += product

    low = 0
    for place, pieces in enumerate(layout):
        own = refs[low : low + 2 * pieces + 1]
        low += 2 * pieces + 1

        @pl.when(which == place)
        def _(own=own):
            run(own[:-1:2], own[1:-1:2], own[-1])

    @pl.when(part == pl.num_programs(2) - 1)
    def _():
        expert = ids_ref[which]
        extra = x[:, MODEL_WIDTH:].astype(F32)
        lane = lax.broadcasted_iota(jnp.int32, extra.shape, 1)
        mine = (lane == expert) | (lane == expert + HALF)
        gate = jnp.sum(jnp.where(mine, extra, 0.0), axis=1, keepdims=True)
        share = acc[...].astype(BF16).astype(F32) * gate

        if len(layout) == 2:

            @pl.when(which == 0)
            def _():
                mix[...] = share

        @pl.when(which == len(layout) - 1)
        def _():
            done = (mix[...] + share if len(layout) == 2 else share).astype(BF16)
            ya_ref[...] = done[:half]
            yb_ref[...] = done[half:]


def experts(ids, xa, xb, weights):
    half_rows, width = xa.shape
    half = min(half_rows, 256)
    tile = 256
    parts = FE // tile
    specs, operands = [], []
    for which, (gate_ups, down) in enumerate(weights):
        if len(weights) == 1:
            at = lambda e, f: f
        elif which == 0:
            at = lambda e, f: jnp.where(e == 0, f, parts - 1)
        else:
            at = lambda e, f: jnp.where(e == 0, 0, f)
        for gate_up in gate_ups:
            shape = (gate_up.shape[0], tile)
            specs += [
                pl.BlockSpec(shape, lambda r, e, f, *_, at=at: (0, at(e, f))),
                pl.BlockSpec(shape, lambda r, e, f, *_, at=at: (0, parts + at(e, f))),
            ]
            operands += [gate_up, gate_up]
        specs.append(pl.BlockSpec((tile, MODEL_WIDTH), lambda r, e, f, *_, at=at: (at(e, f), 0)))
        operands.append(down)
    row_spec = pl.BlockSpec((half, width), lambda r, e, f, *_: (r, 0))
    out_spec = pl.BlockSpec((half, MODEL_WIDTH), lambda r, e, f, *_: (r, 0))
    return pl.pallas_call(
        functools.partial(expert_kernel, tuple(len(pieces) for pieces, _ in weights)),
        grid_spec=pltpu.PrefetchScalarGridSpec(
            num_scalar_prefetch=1,
            grid=(half_rows // half, len(weights), parts),
            in_specs=[row_spec, row_spec] + specs,
            out_specs=[out_spec, out_spec],
            scratch_shapes=[
                pltpu.VMEM((2 * half, width), BF16),
                pltpu.VMEM((2 * half, MODEL_WIDTH), F32),
                pltpu.VMEM((2 * half, MODEL_WIDTH), F32),
            ],
        ),
        out_shape=[jax.ShapeDtypeStruct((half_rows, MODEL_WIDTH), BF16)] * 2,
        compiler_params=params(0, 0, 0),
        cost_estimate=pl.CostEstimate(
            flops=12 * len(weights) * half_rows * MODEL_WIDTH * FE,
            bytes_accessed=6 * len(weights) * MODEL_WIDTH * FE,
            transcendentals=0,
        ),
        name="experts",
    )(ids, xa, xb, *operands)


def mixture(ids, sent, weights, n_bits):
    half = sent.shape[0] // 2
    orders = (list(range(n_bits)), list(reversed(range(n_bits))))
    held = [[sent[:half]], [sent[half:]]]
    arrived = []
    for level in range(n_bits):
        pair = []
        for side in range(2):
            buffers = held[side]
            block = buffers[0] if len(buffers) == 1 else jnp.concatenate(buffers, axis=0)
            pair.append(swapped(block, "req", orders[side][level]))
        for side in range(2):
            held[side].append(pair[side])
        arrived.append(pair)
    here = [jnp.concatenate(held[side][:-1], axis=0) for side in range(2)]
    near = tuple(experts(ids[:1], here[0], here[1], weights[:1]))
    near, far_weights = lax.optimization_barrier((near, weights[1]))
    far = tuple(experts(ids[1:], here[0], here[1], (far_weights,)))
    near, far, last = lax.optimization_barrier((near, far, tuple(arrived[-1])))
    early = [near[side].astype(F32) + far[side].astype(F32) for side in range(2)]
    late = experts(ids, last[0], last[1], weights)
    totals = []
    for side in range(2):
        added = [early[side][:half]]
        waiting, low = [], half
        for level in range(n_bits - 1):
            size = half * 2**level
            waiting.append(early[side][low : low + size])
            low += size
        waiting.append(late[side].astype(F32))
        for level in reversed(range(n_bits)):
            back = swapped(waiting[level].astype(BF16), "req", orders[side][level]).astype(F32)
            added.append(back[:half])
            low = half
            for below in range(level):
                size = half * 2**below
                waiting[below] = waiting[below] + back[low : low + size]
                low += size
        totals.append(functools.reduce(jnp.add, added))
    return jnp.concatenate(totals, axis=0)


def on_device(
    tokens,
    norm1_gain,
    query_key_value_weight,
    w_out,
    norm2_gain,
    router_weight,
    w_gate_up,
    w_down,
    routes,
    key_page_store,
    value_page_store,
    page_table,
    cached_pages,
    anchor,
):
    req_index = lax.axis_index("req")
    head_index = lax.axis_index("head")
    n_groups = lax.axis_size("head")
    req_count = lax.axis_size("req")
    rows = tokens.shape[0]
    req_dev = page_table.shape[0]
    page_size = key_page_store.shape[1]
    group_heads = QUERY_HEADS // n_groups
    kv_index = head_index // (n_groups // KEY_VALUE_HEADS)
    far_bit = req_count.bit_length() - 2
    far_mask = 2**far_bit

    partner = req_index ^ 1
    partner_anchor = lax.dynamic_slice_in_dim(anchor, partner * req_dev, req_dev, 0)
    leaving = partner_anchor // req_dev == req_index
    out_row = jnp.sum(jnp.where(leaving, partner_anchor, 0)) % req_dev
    out_pages = lax.dynamic_index_in_dim(page_table, out_row, 0, keepdims=False)
    half_pages = page_table.shape[1] // 2
    core = head_index % 2
    out_pages = lax.dynamic_slice_in_dim(out_pages, core * half_pages, half_pages, 0)
    left = leaving_pages(out_pages, kv_index, key_page_store, value_page_store)
    tokens, left = lax.optimization_barrier((tokens, left))
    got = swapped(left, "req", 0)

    def share_of(block):
        count = block.shape[0] // n_groups
        return lax.dynamic_slice_in_dim(block, head_index * count, count, 0)

    middle = w_gate_up.shape[1] // 2
    far_down = swapped(share_of(w_down[0]), "req", far_bit)
    far_first = swapped(share_of(w_gate_up[0, :middle]), "req", far_bit)
    far_second = swapped(share_of(w_gate_up[0, middle:]), "req", far_bit)

    first_row = (req_index * n_groups + head_index) * rows
    start = cached_pages[anchor[first_row // REQUEST_TOKENS]] * page_size
    positions = start + first_row % REQUEST_TOKENS + jnp.arange(rows, dtype=jnp.int32)
    frequency = jnp.exp(
        -jnp.log(F32(THETA)) * jnp.arange(HALF, dtype=F32) * 2.0 / HEAD_SIZE
    )
    angles = positions.astype(F32)[:, None] * frequency[None, :]
    cosine, sine = jnp.cos(angles), jnp.sin(angles)
    outgoing, appended = project(
        tokens,
        norm1_gain,
        query_key_value_weight,
        jnp.concatenate([cosine, cosine], axis=1),
        jnp.concatenate([-sine, sine], axis=1),
        n_groups,
    )
    outgoing, got = lax.optimization_barrier((outgoing, got))
    more = swapped(got, "head", 0)
    head_rows = lax.all_to_all(outgoing, "head", split_axis=0, concat_axis=0, tiled=True)
    head_rows, far_down = lax.optimization_barrier((head_rows, far_down))
    far_down = lax.all_gather(far_down, "head", axis=0, tiled=True)
    head_rows = head_rows.reshape(req_dev, REQUEST_TOKENS, outgoing.shape[2])

    slot_anchor = lax.dynamic_slice_in_dim(anchor, req_index * req_dev, req_dev, 0)
    moved = (slot_anchor // req_dev != req_index).astype(jnp.int32)
    pages = page_table[slot_anchor % req_dev]
    info = jnp.concatenate([cached_pages[slot_anchor], moved, jnp.stack([kv_index, core]).astype(jnp.int32)])
    answers = attend(pages, info, head_rows, key_page_store, value_page_store, got, more, group_heads)
    answers = answers.reshape(n_groups, rows, group_heads * HEAD_SIZE)
    answers, far_first = lax.optimization_barrier((answers, far_first))
    far_first = lax.all_gather(far_first, "head", axis=0, tiled=True)
    back = lax.all_to_all(answers, "head", split_axis=0, concat_axis=0, tiled=True)

    back, far_down = lax.optimization_barrier((back, far_down))
    router = jnp.pad(router_weight, ((0, 0), (0, LANES - router_weight.shape[1])))
    residual, sent = settle(tokens, back, w_out, norm2_gain, router, routes)
    sent, far_first, far_second = lax.optimization_barrier((sent, far_first, far_second))
    far_second = lax.all_gather(far_second, "head", axis=0, tiled=True)
    ids = jnp.stack([req_index, req_index ^ far_mask]).astype(jnp.int32)
    weights = (((w_gate_up[0],), w_down[0]), ((far_first, far_second), far_down))
    mixed = (residual + mixture(ids, sent, weights, far_bit)).astype(BF16)
    return (mixed, appended)


def solution(mesh):
    return jax.shard_map(
        on_device,
        mesh=mesh,
        in_specs=(
            P(("req", "head"), None),
            P(),
            P(),
            P(),
            P(),
            P(),
            P("req", None, None),
            P("req", None, None),
            P(("req", "head"), None),
            P("req", None, None),
            P("req", None, None),
            P("req", None),
            P(),
            P(),
        ),
        out_specs=(P(("req", "head"), None), P(("req", "head"), None)),
        check_vma=False,
    )
```
